128 devices in a mesh: tm: 8 (over y, z_hi), rows: 16 (over z_lo, x, core).
Axes of the slice: x: 4, y: 4, z: 4 (z_hi: 2, z_lo: 2; z = z_hi * 2 + z_lo), core: 2. Of those that a mesh axis runs over, the one named last changes fastest.
Arguments:
- clip: bfloat16 [16, 128, 128, 384], P('tm', 'rows'), may hold values from -6 to 6
- gain_one: float32 [384], replicated, may hold values from 0.5 to 1.5
- bias_one: float32 [384], replicated, may hold values from -3 to 3
- kernel_one: bfloat16 [3, 3, 3, 384, 384], replicated, may hold values from -0.0625 to 0.0625
- gain_two: float32 [384], replicated, may hold values from 0.5 to 1.5
- bias_two: float32 [384], replicated, may hold values from -3 to 3
- kernel_two: bfloat16 [3, 3, 3, 384, 384], replicated, may hold values from -0.0625 to 0.0625
- down_kernel: bfloat16 [3, 384, 384], replicated, may hold values from -0.1875 to 0.1875
- down_bias: float32 [384], replicated, may hold values from -3 to 3
Outputs:
- latents: bfloat16 [8, 128, 128, 384], P('tm', None, 'rows')
The draws below stay inside these ranges and needn't reach their ends.
All inputs are finite; a program needn't handle non-finite values.
Results may differ from the reference program's by a relative error of at most 0.0051.
Values may be sent and summed in bfloat16 or wider, within the bound.
No kernel may reach another device: no remote copies, remote signals or barrier semaphores. Data moves between devices by JAX's collectives and lax.ppermute only.
A program may use at most 256 MiB of HBM per device.

```python
import jax
import jax.numpy as jnp
from jax import lax

C = 384
W = 128
FRAMES = 16
HEIGHT = 128


def block_levels(own_key, dims, pieces, smallest, largest):
    def one(axis_at, blocks):
        draws = jax.random.uniform(jax.random.fold_in(jax.random.fold_in(own_key, 6), axis_at), (blocks,), jnp.float32, smallest / len(pieces), largest / len(pieces))
        return jnp.repeat(jnp.exp(draws), dims[axis_at] // blocks).reshape((-1,) + (1,) * (len(dims) - axis_at - 1))

    factor_of = one(*pieces[0])
    for cut in pieces[1:]:
        factor_of = factor_of * one(*cut)
    return factor_of


def noise(key, extent, scale, most, cuts=(), dtype=jnp.bfloat16):
    level = block_levels(key, extent, cuts, -0.22, 0.18) if cuts else 1.0
    array = jax.random.normal(key, extent, jnp.float32) * scale * level
    return jnp.minimum(jnp.maximum(array, -most), most).astype(dtype)


def setup_inputs(seed: int = 0) -> dict:
    key_of = jax.random.split(jax.random.key(seed), 10)
    return {
        "clip": noise(key_of[0], (FRAMES, HEIGHT, W, C), 1.0, 6.0, ((0, 8), (1, 16))),
        "gain_one": jnp.clip(jax.random.uniform(key_of[1], (C,), jnp.float32, 0.5, 1.5), 0.5, 1.5),
        "bias_one": noise(key_of[2], (C,), 0.5, 3.0, (), jnp.float32),
        "kernel_one": noise(key_of[3], (3, 3, 3, C, C), (27 * C) ** -0.5, 0.0625),
        "gain_two": jnp.clip(jax.random.uniform(key_of[4], (C,), jnp.float32, 0.5, 1.5), 0.5, 1.5),
        "bias_two": noise(key_of[5], (C,), 0.5, 3.0, (), jnp.float32),
        "kernel_two": noise(key_of[6], (3, 3, 3, C, C), (27 * C) ** -0.5, 0.0625),
        "down_kernel": noise(key_of[7], (3, C, C), (3 * C) ** -0.5, 0.1875),
        "down_bias": noise(key_of[8], (C,), 0.5, 3.0, (), jnp.float32),
    }


EPS = 1e-06

def activate(value, gain):
    square = lax.optimization_barrier(jnp.mean(value * value, axis=-1, keepdims=True))
    scaled = value * lax.rsqrt(square + EPS) * gain
    return jax.nn.silu(scaled)

def conv_whole(active, kernel):
    frame_count, row_count, width, chans = active.shape
    padded = jnp.pad(active.astype(jnp.float32), ((2, 0), (1, 1), (1, 1), (0, 0)))
    trio = jnp.concatenate([padded[:, :, 0:width], padded[:, :, 1:width + 1], padded[:, :, 2:width + 2]], axis=3)
    flat = kernel.astype(jnp.float32).reshape(3, 3, 3 * chans, chans)
    total = jnp.zeros((frame_count, row_count, width, chans), jnp.float32)
    for tap_time in range(3):
        for tap_row in range(3):
            piece = trio[tap_time:tap_time + frame_count, tap_row:tap_row + row_count]
            total = total + jnp.einsum('frwc,cd->frwd', piece, flat[tap_time, tap_row], precision=lax.Precision.HIGHEST)
    return total

def reference(clip, gain_one, bias_one, kernel_one, gain_two, bias_two, kernel_two, down_kernel, down_bias):
    clip_float = clip.astype(jnp.float32)
    first = activate(clip_float, gain_one).astype(jnp.bfloat16)
    hidden = conv_whole(first, kernel_one) + bias_one
    second = activate(hidden, gain_two).astype(jnp.bfloat16)
    block = (conv_whole(second, kernel_two) + bias_two + clip_float).astype(jnp.bfloat16)
    block_float = block.astype(jnp.float32)
    evens = block_float[0::2]
    odds = block_float[1::2]
    earlier = jnp.concatenate([jnp.zeros_like(odds[:1]), odds[:-1]], axis=0)
    down = down_kernel.astype(jnp.float32)
    total = jnp.einsum('frwc,cd->frwd', earlier, down[0], precision=lax.Precision.HIGHEST)
    total = total + jnp.einsum('frwc,cd->frwd', evens, down[1], precision=lax.Precision.HIGHEST)
    total = total + jnp.einsum('frwc,cd->frwd', odds, down[2], precision=lax.Precision.HIGHEST)
    return (total + down_bias).astype(jnp.bfloat16)
```

```python
import jax
import jax.numpy as jnp
from jax import lax
from jax.experimental import pallas as pl
from jax.experimental.pallas import tpu as pltpu
from jax.sharding import PartitionSpec as P

EPS = 1e-06
C = 384
BF = jnp.bfloat16
F32 = jnp.float32


def activate(value, gain):
    square = jnp.mean(value * value, axis=-1, keepdims=True)
    scaled = value * lax.rsqrt(square + EPS) * gain
    return scaled / (1.0 + jnp.exp(-scaled))


def earlier(value):
    rank = value.ndim
    index = lax.broadcasted_iota(jnp.int32, value.shape, rank - 2)
    return jnp.where(index == 0, 0.0, pltpu.roll(value, 1, rank - 2))


def transformed(even, odd):
    even_before, odd_before = earlier(even), earlier(odd)
    return even_before - even, odd_before + even, even - odd_before, odd_before - odd


def kernel_body(
    pos_ref, clip_ref, g1_ref, b1_ref, g2_ref, b2_ref, dk_ref, db_ref, u1_hbm, u2_hbm,
    out_ref, u1_ref, u2_ref, d1_ref, d2_ref, s_ref, sems,
):
    copy_one = pltpu.make_async_copy(u1_hbm, u1_ref, sems.at[0])
    copy_two = pltpu.make_async_copy(u2_hbm, u2_ref, sems.at[1])
    copy_one.start()
    copy_two.start()

    def prepare_one(r, carry):
        x = activate(clip_ref[r].astype(F32), g1_ref[...]).astype(BF).astype(F32)
        for q, d in enumerate(transformed(x[:, :8], x[:, 8:])):
            d1_ref[q, r] = jnp.concatenate([d[0:11], d[9:20]], axis=1).astype(BF)
        return carry

    lax.fori_loop(0, 12, prepare_one, 0)
    copy_one.wait()

    def products(d_ref, u_ref, r, rows, width):
        m = []
        for q in range(4):
            lhs = jnp.concatenate(
                [
                    d_ref[q, pl.ds(r + i, rows), j : j + width].reshape(rows * width * 16, C)
                    for i in range(3)
                    for j in range(3)
                ],
                axis=1,
            )
            rhs = u_ref[q].reshape(9 * C, C)
            m.append(jnp.dot(lhs, rhs, preferred_element_type=F32))
        total, diff = m[1] + m[2], m[1] - m[2]
        return m[0] + total, diff - m[3]

    row0 = pos_ref[1] * 8 - 1
    col0 = pos_ref[0] * 16 - 1

    def conv_one(block, carry):
        r = block * 2
        col = lax.broadcasted_iota(jnp.int32, (2, 9, 8, 1), 1) + col0
        row = lax.broadcasted_iota(jnp.int32, (2, 9, 8, 1), 0) + (row0 + r)
        row_ok = (row >= 0) & (row < 128)
        for parity, h in enumerate(products(d1_ref, u1_ref, r, 2, 9)):
            act = activate(h + b1_ref[...], g2_ref[...]).astype(BF).astype(F32)
            act = act.reshape(2, 9, 2, 8, C)
            for half in range(2):
                column = col + 9 * half
                ok = row_ok & (column >= 0) & (column < 128)
                s_ref[parity, pl.ds(r, 2), 9 * half : 9 * half + 9] = jnp.where(ok, act[:, :, half], 0.0)
        return carry

    lax.fori_loop(0, 5, conv_one, 0)

    def prepare_two(r, carry):
        for q, d in enumerate(transformed(s_ref[0, r], s_ref[1, r])):
            d2_ref[q, r] = jnp.concatenate([d[0:10], d[8:18]], axis=1).astype(BF)
        return carry

    lax.fori_loop(0, 10, prepare_two, 0)
    copy_two.wait()

    def conv_two(block, carry):
        r = block * 2
        clip = clip_ref[pl.ds(r + 2, 2)].astype(F32)
        blocks = []
        for parity, h in enumerate(products(d2_ref, u2_ref, r, 2, 8)):
            part = clip[:, :, 8 * parity : 8 * parity + 8]
            part = jnp.concatenate([part[:, 2:10], part[:, 10:18]], axis=2).reshape(256, C)
            blocks.append((h + b2_ref[...] + part).astype(BF).astype(F32))
        even, odd = blocks
        before = earlier(odd.reshape(32, 8, C)).reshape(256, C)
        lhs = jnp.concatenate([before.astype(BF), even.astype(BF), odd.astype(BF)], axis=1)
        latent = jnp.dot(lhs, dk_ref[...], preferred_element_type=F32) + db_ref[...]
        out_ref[pl.ds(r, 2)] = latent.astype(BF).reshape(2, 8, 16, C)
        return carry

    lax.fori_loop(0, 4, conv_two, 0)


def weights(kernel):
    k = kernel.reshape(3, 9, C, C)
    k0, k1, k2 = (k[t].astype(F32) for t in range(3))
    outer = k0 + k2
    return jnp.stack([k[0], (0.5 * (outer + k1)).astype(BF), (0.5 * (outer - k1)).astype(BF), k[2]])


def body(
    clip, gain_one, bias_one, kernel_one, gain_two, bias_two, kernel_two, down_kernel, down_bias
):
    pos = jnp.stack([lax.axis_index("tm"), lax.axis_index("rows")]).astype(jnp.int32)
    wide = jnp.pad(clip, ((0, 0), (0, 0), (2, 2), (0, 0)))
    pieces = jnp.stack([wide[:, :, 16 * d : 16 * d + 20] for d in range(8)])
    got = lax.all_to_all(pieces.reshape(8, 320, C), "tm", 0, 0, tiled=True)
    own = got.reshape(8, 2, 8, 20, C).transpose(2, 3, 1, 0, 4).reshape(8, 20, 16, C)
    forward = [(i, i + 1) for i in range(15)]
    backward = [(i + 1, i) for i in range(15)]
    above = lax.ppermute(own[6:8], "rows", forward)
    below = lax.ppermute(own[0:2], "rows", backward)
    patch = jnp.concatenate([above, own, below], axis=0)

    vmem = pl.BlockSpec(memory_space=pltpu.VMEM)
    hbm = pl.BlockSpec(memory_space=pl.ANY)
    latent = pl.pallas_call(
        kernel_body,
        out_shape=jax.ShapeDtypeStruct((8, 8, 16, C), BF),
        in_specs=[pl.BlockSpec(memory_space=pltpu.SMEM)] + [vmem] * 7 + [hbm] * 2,
        out_specs=vmem,
        scratch_shapes=[
            pltpu.VMEM((4, 9, C, C), BF),
            pltpu.VMEM((4, 9, C, C), BF),
            pltpu.VMEM((4, 12, 11, 16, C), BF),
            pltpu.VMEM((4, 10, 10, 16, C), BF),
            pltpu.VMEM((2, 10, 18, 8, C), F32),
            pltpu.SemaphoreType.DMA((2,)),
        ],
        compiler_params=pltpu.CompilerParams(vmem_limit_bytes=60 * 2**20),
        name="block",
    )(
        pos, patch, gain_one.reshape(1, C), bias_one.reshape(1, C), gain_two.reshape(1, C),
        bias_two.reshape(1, C), down_kernel.reshape(3 * C, C), down_bias.reshape(1, C),
        weights(kernel_one), weights(kernel_two),
    )
    send = latent.reshape(8, 8, 2, 8, C).transpose(3, 2, 0, 1, 4).reshape(8, 128, C)
    send = lax.all_to_all(send, "tm", 0, 0, tiled=True)
    send = lax.all_to_all(send.reshape(16, 64, C), "rows", 0, 0, tiled=True)
    return send.reshape(1, 128, 8, C)


def solution(mesh):
    return jax.shard_map(
        body,
        mesh=mesh,
        in_specs=(P("tm", "rows", None, None), P(), P(), P(), P(), P(), P(), P(), P()),
        out_specs=P("tm", None, "rows", None),
        check_vma=False,
    )
```

```python
import jax
import jax.numpy as jnp
from jax import lax
from jax.experimental import pallas as pl
from jax.experimental.pallas import tpu as pltpu
from jax.sharding import PartitionSpec as P

EPS = 1e-06
C = 384
BF = jnp.bfloat16
F32 = jnp.float32


def activate(value, gain):
    square = jnp.mean(value * value, axis=-1, keepdims=True)
    scaled = value * lax.rsqrt(square + EPS) * gain
    half = 0.5 * scaled
    return half + half * jnp.tanh(half)


def earlier(value):
    rank = value.ndim
    index = lax.broadcasted_iota(jnp.int32, value.shape, rank - 2)
    return jnp.where(index == 0, 0.0, pltpu.roll(value, 1, rank - 2))


def transformed(even, odd):
    even_before, odd_before = earlier(even), earlier(odd)
    return even_before - even, odd_before + even, even - odd_before, odd_before - odd


GROUPS = (((0, 1), 0), ((2, 3, 4, 5), 80), ((6, 7), 240))


def pack_body(clip_ref, out_ref, halo_ref):
    zero = jnp.zeros((2, C), F32)
    for d in range(8):
        for rows, base in GROUPS:
            count = 2 * len(rows)
            for k in range(count):
                f, r = k // len(rows), rows[k % len(rows)]
                out_ref[d, base + 16 * k : base + 16 * k + 16] = clip_ref[f, r, 16 * d : 16 * d + 16]
                left, right = zero, zero
                if d > 0:
                    left = clip_ref[f, r, 16 * d - 16 : 16 * d].astype(F32)[14:16]
                if d < 7:
                    right = clip_ref[f, r, 16 * d + 16 : 16 * d + 32].astype(F32)[0:2]
                halo_ref[4 * k : 4 * k + 2] = left
                halo_ref[4 * k + 2 : 4 * k + 4] = right
            start = base + 16 * count
            out_ref[d, start : start + 4 * count] = halo_ref[0 : 4 * count].astype(BF)


STRIDE = 12 * 2 * 24
PLACE = [16, 17] + list(range(16)) + [18, 19]


def kernel_body(
    above_ref, own_ref, below_ref, g1_ref, b1_ref, g2_ref, b2_ref, db_ref, dk_ref,
    u1_hbm, u2_hbm,
    out_ref, u1_ref, u2_ref, x_ref, d1_ref, d2_ref, s_ref, l_ref, sems,
):
    copy_one = pltpu.make_async_copy(u1_hbm, u1_ref, sems.at[0])
    copy_two = pltpu.make_async_copy(u2_hbm, u2_ref, sems.at[1])
    copy_one.start()
    g1, b1, g2, b2, db = (ref[...].reshape(1, C) for ref in (g1_ref, b1_ref, g2_ref, b2_ref, db_ref))

    def unpack(source, carry):
        for ref, base, first, rows in (
            (above_ref, 0, 0, 2), (own_ref, 0, 2, 2), (own_ref, 80, 4, 4),
            (own_ref, 240, 8, 2), (below_ref, 0, 10, 2),
        ):
            halo = ref[source, base + 32 * rows : base + 40 * rows].astype(F32)
            for k in range(2 * rows):
                f, r = k // rows, first + k % rows
                at = pl.multiple_of(source * STRIDE + (2 * r + f) * 24, 8)
                main = ref[source, base + 16 * k : base + 16 * k + 16].astype(F32)
                for n in range(3):
                    x_ref[n, pl.ds(at, 16)] = main[:, 128 * n : 128 * n + 128]
                    x_ref[n, pl.ds(at + 16, 4)] = halo[4 * k : 4 * k + 4, 128 * n : 128 * n + 128]
        return carry

    lax.fori_loop(0, 8, unpack, 0)

    def cells(r, parity, columns):
        start = (2 * r + parity) * 24
        parts = [
            jnp.stack([x_ref[n, pl.ds(start + PLACE[w], 8, stride=STRIDE)] for w in columns])
            for n in range(3)
        ]
        return jnp.concatenate(parts, axis=2)

    def prepare_one(r, carry):
        halves = [
            activate(cells(r, parity, range(20)), g1).astype(BF).astype(F32) for parity in range(2)
        ]
        for q, d in enumerate(transformed(*halves)):
            d1_ref[q, r] = jnp.concatenate([d[0:11], d[9:20]], axis=1).astype(BF)
        return carry

    lax.fori_loop(0, 12, prepare_one, 0)
    copy_one.wait()
    copy_two.start()

    def products(d_ref, u_ref, r, rows, width):
        m = []
        count = rows * width * 16
        for q in range(4):
            def piece(i, first, span):
                return d_ref[q, pl.ds(r + i, rows), first : first + span].reshape(rows * span * 16, C)

            taps = [(i, j) for i in range(3) for j in range(3)]
            lhs = jnp.concatenate([piece(i, j, width) for i, j in taps], axis=1)
            main = jnp.dot(lhs, u_ref[q, :, :, :256].reshape(9 * C, 256), preferred_element_type=F32)
            lhs = jnp.concatenate([piece(i, 0, width + 1) for i in range(3)], axis=1)
            rhs = jnp.concatenate(
                [
                    jnp.concatenate([u_ref[q, 3 * i + j, :, 256:] for j in range(2)], axis=1)
                    for i in range(3)
                ],
                axis=0,
            )
            pair = jnp.dot(lhs, rhs, preferred_element_type=F32).reshape(rows, width + 1, 16, 256)
            lhs = jnp.concatenate([piece(i, 2, width) for i in range(3)], axis=1)
            rhs = jnp.concatenate([u_ref[q, 3 * i + 2, :, 256:] for i in range(3)], axis=0)
            last = jnp.dot(lhs, rhs, preferred_element_type=F32)
            rest = pair[:, :width, :, :128] + pair[:, 1:, :, 128:]
            rest = rest.reshape(count, 128) + last
            m.append(jnp.concatenate([main, rest], axis=1))
        total, diff = m[1] + m[2], m[1] - m[2]
        return m[0] + total, diff - m[3]

    row0 = lax.axis_index("rows") * 8 - 1
    col0 = lax.axis_index("tm") * 16 - 1

    def conv_one(block, carry):
        r = block * 2
        col = lax.broadcasted_iota(jnp.int32, (2, 9, 8, 1), 1) + col0
        row = lax.broadcasted_iota(jnp.int32, (2, 9, 8, 1), 0) + (row0 + r)
        row_ok = (row >= 0) & (row < 128)
        for parity, h in enumerate(products(d1_ref, u1_ref, r, 2, 9)):
            act = activate(h + b1, g2)
            act = act.reshape(2, 9, 2, 8, C)
            for half in range(2):
                column = col + 9 * half
                ok = row_ok & (column >= 0) & (column < 128)
                s_ref[parity, pl.ds(r, 2), 9 * half : 9 * half + 9] = jnp.where(ok, act[:, :, half], 0.0)
        return carry

    lax.fori_loop(0, 5, conv_one, 0)

    def prepare_two(r, carry):
        for q, d in enumerate(transformed(s_ref[0, r], s_ref[1, r])):
            d2_ref[q, r] = jnp.concatenate([d[0:10], d[8:18]], axis=1).astype(BF)
        return carry

    lax.fori_loop(0, 10, prepare_two, 0)
    copy_two.wait()

    def conv_two(block, carry):
        r = block * 2
        blocks = []
        for parity, h in enumerate(products(d2_ref, u2_ref, r, 2, 8)):
            part = jnp.stack([cells(r + 2 + k, parity, range(2, 18)) for k in range(2)])
            part = jnp.concatenate([part[:, 0:8], part[:, 8:16]], axis=2).reshape(256, C)
            blocks.append((h + b2 + part).astype(BF).astype(F32))
        even, odd = blocks
        before = earlier(odd.reshape(32, 8, C)).reshape(256, C)
        lhs = jnp.concatenate([before.astype(BF), even.astype(BF), odd.astype(BF)], axis=1)
        latent = jnp.dot(lhs, dk_ref[...], preferred_element_type=F32) + db
        for n in range(3):
            l_ref[n] = latent[:, 128 * n : 128 * n + 128]
        for j in range(8):
            for half in range(2):
                at = pl.multiple_of(64 * half + 8 * r, 16)
                for n in range(3):
                    rows = [l_ref[n, pl.ds(128 * k + 8 * half + j, 8, stride=16)] for k in range(2)]
                    out_ref[j, pl.ds(at, 16), 128 * n : 128 * n + 128] = jnp.concatenate(rows, axis=0).astype(BF)
        return carry

    lax.fori_loop(0, 4, conv_two, 0)


def weights_body(one_ref, two_ref, u1_ref, u2_ref):
    for k_ref, u_ref in ((one_ref, u1_ref), (two_ref, u2_ref)):
        outer = k_ref[0, 0].astype(F32) + k_ref[2, 0].astype(F32)
        middle = k_ref[1, 0].astype(F32)
        u_ref[0, 0] = k_ref[0, 0]
        u_ref[1, 0] = (0.5 * (outer + middle)).astype(BF)
        u_ref[2, 0] = (0.5 * (outer - middle)).astype(BF)
        u_ref[3, 0] = k_ref[2, 0]


def weights(kernel_one, kernel_two):
    return pl.pallas_call(
        weights_body,
        grid=(9,),
        out_shape=[jax.ShapeDtypeStruct((4, 9, C, C), BF)] * 2,
        in_specs=[pl.BlockSpec((3, 1, C, C), lambda n: (0, n, 0, 0))] * 2,
        out_specs=[pl.BlockSpec((4, 1, C, C), lambda n: (0, n, 0, 0))] * 2,
        compiler_params=pltpu.CompilerParams(vmem_limit_bytes=60 * 2**20),
        cost_estimate=pl.CostEstimate(flops=16000000, bytes_accessed=37000000, transcendentals=0),
        name="weights",
    )(kernel_one.reshape(3, 9, C, C), kernel_two.reshape(3, 9, C, C))


def block_call(above, own, below, vectors, down_kernel, u1, u2):
    vmem = pl.BlockSpec(memory_space=pltpu.VMEM)
    hbm = pl.BlockSpec(memory_space=pl.ANY)
    return pl.pallas_call(
        kernel_body,
        out_shape=jax.ShapeDtypeStruct((8, 128, C), BF),
        in_specs=[vmem] * 9 + [hbm] * 2,
        out_specs=vmem,
        scratch_shapes=[
            pltpu.VMEM((4, 9, C, C), BF),
            pltpu.VMEM((4, 9, C, C), BF),
            pltpu.VMEM((3, 8 * STRIDE, 128), F32),
            pltpu.VMEM((4, 12, 11, 16, C), BF),
            pltpu.VMEM((4, 10, 10, 16, C), BF),
            pltpu.VMEM((2, 10, 18, 8, C), F32),
            pltpu.VMEM((3, 256, 128), F32),
            pltpu.SemaphoreType.DMA((2,)),
        ],
        compiler_params=pltpu.CompilerParams(vmem_limit_bytes=60 * 2**20),
        name="block",
    )(above, own, below, *vectors, down_kernel.reshape(3 * C, C), u1, u2)


def body(
    clip, gain_one, bias_one, kernel_one, gain_two, bias_two, kernel_two, down_kernel, down_bias
):
    vmem = pl.BlockSpec(memory_space=pltpu.VMEM)
    pieces = pl.pallas_call(
        pack_body,
        out_shape=jax.ShapeDtypeStruct((8, 320, C), BF),
        in_specs=[vmem],
        out_specs=vmem,
        scratch_shapes=[pltpu.VMEM((32, C), F32)],
        compiler_params=pltpu.CompilerParams(vmem_limit_bytes=16 * 2**20),
        name="pack",
    )(clip)
    u1, u2 = weights(kernel_one, kernel_two)
    own = lax.all_to_all(pieces, "tm", 0, 0, tiled=True)
    own, u1, u2 = lax.optimization_barrier((own, u1, u2))
    above = lax.ppermute(own[:, 240:], "rows", [(i, i + 1) for i in range(15)])
    below = lax.ppermute(own[:, :80], "rows", [(i + 1, i) for i in range(15)])
    vectors = (gain_one, bias_one, gain_two, bias_two, down_bias)
    latent = block_call(above, own, below, vectors, down_kernel, u1, u2)
    send = lax.all_to_all(latent, "tm", 0, 0, tiled=True)
    send = lax.all_to_all(send.reshape(16, 64, C), "rows", 0, 0, tiled=True)
    return send.reshape(1, 128, 8, C)


def solution(mesh):
    return jax.shard_map(
        body,
        mesh=mesh,
        in_specs=(P("tm", "rows", None, None), P(), P(), P(), P(), P(), P(), P(), P()),
        out_specs=P("tm", None, "rows", None),
        check_vma=False,
    )
```

```python
import jax
import jax.numpy as jnp
from jax import lax
from jax.experimental import pallas as pl
from jax.experimental.pallas import tpu as pltpu
from jax.sharding import PartitionSpec as P

EPS = 1e-06
C = 384
BF = jnp.bfloat16
F32 = jnp.float32


def activate(value, gain):
    square = jnp.mean(value * value, axis=-1, keepdims=True)
    scaled = value * lax.rsqrt(square + EPS) * gain
    half = 0.5 * scaled
    return half + half * jnp.tanh(half)


def earlier(value):
    rank = value.ndim
    index = lax.broadcasted_iota(jnp.int32, value.shape, rank - 2)
    return jnp.where(index == 0, 0.0, pltpu.roll(value, 1, rank - 2))


def transformed(even, odd):
    even_before, odd_before = earlier(even), earlier(odd)
    return even_before - even, odd_before + even, even - odd_before, odd_before - odd


GROUPS = (((0, 1), 0, 0), ((2, 3), 1, 0), ((4, 5), 1, 80), ((6, 7), 0, 80))


def pack_body(clip_ref, edge_ref, mid_ref, halo_ref):
    zero = jnp.zeros((2, C), F32)
    for d in range(8):
        for rows, which, base in GROUPS:
            out_ref = (edge_ref, mid_ref)[which]
            count = 2 * len(rows)
            for k in range(count):
                f, r = k // len(rows), rows[k % len(rows)]
                out_ref[d, base + 16 * k : base + 16 * k + 16] = clip_ref[f, r, 16 * d : 16 * d + 16]
                left, right = zero, zero
                if d > 0:
                    left = clip_ref[f, r, 16 * d - 16 : 16 * d].astype(F32)[14:16]
                if d < 7:
                    right = clip_ref[f, r, 16 * d + 16 : 16 * d + 32].astype(F32)[0:2]
                halo_ref[4 * k : 4 * k + 2] = left
                halo_ref[4 * k + 2 : 4 * k + 4] = right
            start = base + 16 * count
            out_ref[d, start : start + 4 * count] = halo_ref[0 : 4 * count].astype(BF)


VMEM_LIMIT = 60 * 2**20


def fetch(k_hbm, v_hbm, u_ref, sems, first):
    pairs = ((k_hbm.at[0], u_ref.at[0]), (v_hbm, u_ref.at[1:3]), (k_hbm.at[2], u_ref.at[3]))
    return [
        pltpu.make_async_copy(source, target, sems.at[first + n])
        for n, (source, target) in enumerate(pairs)
    ]


def reordered(source_of):
    place = lax.broadcasted_iota(jnp.int32, (256, 256), 0)
    source = lax.broadcasted_iota(jnp.int32, (256, 256), 1)
    return jnp.where(source_of(place) == source, 1.0, 0.0).astype(BF)


def unpack(x_ref, chunks):
    order = reordered(lambda k: (k // 128) * 128 + (k % 8) * 16 + (k % 128) // 8)
    for n in range(0, len(chunks), 2):
        rows = [chunk(source) for chunk in chunks[n : n + 2] for source in range(8)]
        moved = jnp.dot(order, jnp.concatenate(rows, axis=0), preferred_element_type=F32)
        x_ref[16 * n : 16 * n + 32] = moved.reshape(32, 8, C)


def chunks_of(ref, first, last):
    return [lambda source, at=at: ref[source, at : at + 16] for at in range(first, last, 16)]


def chosen(condition, ref, other_ref):
    return [
        lambda source, at=at: jnp.where(condition, ref[source, at : at + 16], other_ref[source, at : at + 16])
        for at in range(0, 80, 16)
    ]


def cells(x_ref, r, parity, halo):
    line = 2 * parity + r % 2
    main = x_ref[pl.ds(80 * (r // 2) + 16 * line, 16)]
    if not halo:
        return main
    at = 80 * (r // 2) + 64 + 4 * line
    return jnp.concatenate([x_ref[pl.ds(at, 2)], main, x_ref[pl.ds(at + 2, 2)]], axis=0)


def prepare_one(x_ref, d_ref, g1):
    def one(r, carry):
        halves = [
            activate(cells(x_ref, r, parity, True), g1).astype(BF).astype(F32)
            for parity in range(2)
        ]
        for q, d in enumerate(transformed(*halves)):
            d_ref[q, r] = jnp.concatenate([d[0:11], d[9:20]], axis=1).astype(BF)
        return carry

    lax.fori_loop(0, 8, one, 0)


def products(d_ref, u_ref, r, rows, width):
    m = []
    count = rows * width * 16
    for q in range(4):
        def piece(i, first, span):
            return d_ref[q, pl.ds(r + i, rows), first : first + span].reshape(rows * span * 16, C)

        taps = [(i, j) for i in range(3) for j in range(3)]
        lhs = jnp.concatenate([piece(i, j, width) for i, j in taps], axis=1)
        main = jnp.dot(lhs, u_ref[q, :, :, :256].reshape(9 * C, 256), preferred_element_type=F32)
        lhs = jnp.concatenate([piece(i, 0, width + 1) for i in range(3)], axis=1)
        rhs = jnp.concatenate(
            [
                jnp.concatenate([u_ref[q, 3 * i + j, :, 256:] for j in range(2)], axis=1)
                for i in range(3)
            ],
            axis=0,
        )
        pair = jnp.dot(lhs, rhs, preferred_element_type=F32).reshape(rows, width + 1, 16, 256)
        lhs = jnp.concatenate([piece(i, 2, width) for i in range(3)], axis=1)
        rhs = jnp.concatenate([u_ref[q, 3 * i + 2, :, 256:] for i in range(3)], axis=0)
        last = jnp.dot(lhs, rhs, preferred_element_type=F32)
        rest = pair[:, :width, :, :128] + pair[:, 1:, :, 128:]
        m.append(jnp.concatenate([main, rest.reshape(count, 128) + last], axis=1))
    total, diff = m[1] + m[2], m[1] - m[2]
    return m[0] + total, diff - m[3]


def conv_one(d_ref, d_row, u_ref, b1, g2, s_ref, s_row, o):
    col = lax.broadcasted_iota(jnp.int32, (2, 9, 8, 1), 1) + (lax.axis_index("tm") * 16 - 1)
    row = lax.broadcasted_iota(jnp.int32, (2, 9, 8, 1), 0) + (lax.axis_index("rows") * 8 - 1 + o)
    row_ok = (row >= 0) & (row < 128)
    for parity, h in enumerate(products(d_ref, u_ref, d_row, 2, 9)):
        act = activate(h + b1, g2).reshape(2, 9, 2, 8, C)
        for half in range(2):
            column = col + 9 * half
            ok = row_ok & (column >= 0) & (column < 128)
            s_ref[parity, pl.ds(s_row, 2), 9 * half : 9 * half + 9] = jnp.where(ok, act[:, :, half], 0.0)


def edges_body(
    above_ref, edge_ref, below_ref, cross_ref, g1_ref, b1_ref, g2_ref, k1_hbm, v1_hbm,
    s_ref, u1_ref, x_ref, d1_ref, sems,
):
    copies = fetch(k1_hbm, v1_hbm, u1_ref, sems, 0)
    for copy in copies:
        copy.start()
    g1, b1, g2 = (ref[...].reshape(1, C) for ref in (g1_ref, b1_ref, g2_ref))
    me = lax.axis_index("rows")
    unpack(
        x_ref,
        chosen(me == 8, cross_ref, above_ref)
        + chunks_of(edge_ref, 0, 160)
        + chosen(me == 7, cross_ref, below_ref),
    )
    prepare_one(x_ref, d1_ref, g1)
    for copy in copies:
        copy.wait()

    def step(block, carry):
        conv_one(d1_ref, 4 * block, u1_ref, b1, g2, s_ref, 2 * block, 8 * block)
        return carry

    lax.fori_loop(0, 2, step, 0)


def block_body(
    edge_ref, mid_ref, g1_ref, b1_ref, g2_ref, b2_ref, db_ref,
    dk_hbm, s_hbm, k1_hbm, v1_hbm, k2_hbm, v2_hbm,
    out_ref, u1_ref, u2_ref, dk_ref, x_ref, d1_ref, d2_ref, s_ref, sems,
):
    copies_one = fetch(k1_hbm, v1_hbm, u1_ref, sems, 0)
    copies_two = fetch(k2_hbm, v2_hbm, u2_ref, sems, 3) + [
        pltpu.make_async_copy(dk_hbm, dk_ref, sems.at[6]),
        pltpu.make_async_copy(s_hbm.at[:, 0:2], s_ref.at[:, 0:2], sems.at[7]),
        pltpu.make_async_copy(s_hbm.at[:, 2:4], s_ref.at[:, 8:10], sems.at[8]),
    ]
    for copy in copies_one:
        copy.start()
    vectors = (g1_ref, b1_ref, g2_ref, b2_ref, db_ref)
    g1, b1, g2, b2, db = (ref[...].reshape(1, C) for ref in vectors)
    unpack(x_ref, chunks_of(edge_ref, 0, 80) + chunks_of(mid_ref, 0, 160) + chunks_of(edge_ref, 80, 160))
    order = reordered(lambda k: (k // 8 % 2) * 128 + (k % 8) * 16 + (k // 16 % 2) * 8 + k // 32)
    prepare_one(x_ref, d1_ref, g1)
    for copy in copies_one:
        copy.wait()
    for copy in copies_two:
        copy.start()

    def step_one(block, carry):
        conv_one(d1_ref, 2 * block, u1_ref, b1, g2, s_ref, 2 * block + 2, 2 * block + 2)
        return carry

    lax.fori_loop(0, 3, step_one, 0)
    for copy in copies_two:
        copy.wait()

    def prepare_two(r, carry):
        for q, d in enumerate(transformed(s_ref[0, r], s_ref[1, r])):
            d2_ref[q, r] = jnp.concatenate([d[0:10], d[8:18]], axis=1).astype(BF)
        return carry

    lax.fori_loop(0, 10, prepare_two, 0)

    def step_two(block, carry):
        r = block * 2
        blocks = []
        for parity, h in enumerate(products(d2_ref, u2_ref, r, 2, 8)):
            part = jnp.stack([cells(x_ref, r + k, parity, False) for k in range(2)])
            part = jnp.concatenate([part[:, 0:8], part[:, 8:16]], axis=2).reshape(256, C)
            blocks.append((h + b2 + part).astype(BF).astype(F32))
        even, odd = blocks
        before = earlier(odd.reshape(32, 8, C)).reshape(256, C)
        lhs = jnp.concatenate([before.astype(BF), even.astype(BF), odd.astype(BF)], axis=1)
        latent = jnp.dot(lhs, dk_ref[...], preferred_element_type=F32) + db
        latent = jnp.dot(order, latent.astype(BF), preferred_element_type=F32).astype(BF)
        for j in range(8):
            for half in range(2):
                at = pl.multiple_of(64 * half + 8 * r, 16)
                out_ref[j, pl.ds(at, 16)] = latent[32 * j + 16 * half : 32 * j + 16 * half + 16]
        return carry

    lax.fori_loop(0, 4, step_two, 0)


def mixed_body(k1_ref, k2_ref, v1_ref, v2_ref):
    for k_ref, v_ref in ((k1_ref, v1_ref), (k2_ref, v2_ref)):
        for n in range(3):
            outer = 0.5 * (k_ref[0, n].astype(F32) + k_ref[2, n].astype(F32))
            middle = 0.5 * k_ref[1, n].astype(F32)
            v_ref[0, n] = (outer + middle).astype(BF)
            v_ref[1, n] = (outer - middle).astype(BF)


def mixed_call(k1, k2):
    return pl.pallas_call(
        mixed_body,
        grid=(3,),
        out_shape=[jax.ShapeDtypeStruct((2, 9, C, C), BF)] * 2,
        in_specs=[pl.BlockSpec((3, 3, C, C), lambda n: (0, n, 0, 0))] * 2,
        out_specs=[pl.BlockSpec((2, 3, C, C), lambda n: (0, n, 0, 0))] * 2,
        compiler_params=pltpu.CompilerParams(vmem_limit_bytes=VMEM_LIMIT),
        cost_estimate=pl.CostEstimate(flops=16000000, bytes_accessed=27000000, transcendentals=0),
        name="mixed",
    )(k1, k2)


VMEM = pl.BlockSpec(memory_space=pltpu.VMEM)
HBM = pl.BlockSpec(memory_space=pl.ANY)


def edges_call(above, edge, below, cross, g1, b1, g2, k1, v1):
    return pl.pallas_call(
        edges_body,
        out_shape=jax.ShapeDtypeStruct((2, 4, 18, 8, C), F32),
        in_specs=[VMEM] * 7 + [HBM] * 2,
        out_specs=VMEM,
        scratch_shapes=[
            pltpu.VMEM((4, 9, C, C), BF),
            pltpu.VMEM((320, 8, C), F32),
            pltpu.VMEM((4, 8, 11, 16, C), BF),
            pltpu.SemaphoreType.DMA((3,)),
        ],
        compiler_params=pltpu.CompilerParams(vmem_limit_bytes=VMEM_LIMIT),
        cost_estimate=pl.CostEstimate(flops=10**10, bytes_accessed=15000000, transcendentals=0),
        name="edges",
    )(above, edge, below, cross, g1, b1, g2, k1, v1)


def block_call(edge, mid, vectors, dk, s, k1, v1, k2, v2):
    return pl.pallas_call(
        block_body,
        out_shape=jax.ShapeDtypeStruct((8, 128, C), BF),
        in_specs=[VMEM] * 7 + [HBM] * 6,
        out_specs=VMEM,
        scratch_shapes=[
            pltpu.VMEM((4, 9, C, C), BF),
            pltpu.VMEM((4, 9, C, C), BF),
            pltpu.VMEM((3 * C, C), BF),
            pltpu.VMEM((320, 8, C), F32),
            pltpu.VMEM((4, 8, 11, 16, C), BF),
            pltpu.VMEM((4, 10, 10, 16, C), BF),
            pltpu.VMEM((2, 10, 18, 8, C), F32),
            pltpu.SemaphoreType.DMA((9,)),
        ],
        compiler_params=pltpu.CompilerParams(vmem_limit_bytes=VMEM_LIMIT),
        cost_estimate=pl.CostEstimate(flops=3 * 10**10, bytes_accessed=28000000, transcendentals=0),
        name="block",
    )(edge, mid, *vectors, dk, s, k1, v1, k2, v2)


def body(
    clip, gain_one, bias_one, kernel_one, gain_two, bias_two, kernel_two, down_kernel, down_bias
):
    edge, mid = pl.pallas_call(
        pack_body,
        out_shape=[jax.ShapeDtypeStruct((8, 160, C), BF)] * 2,
        in_specs=[VMEM],
        out_specs=[VMEM] * 2,
        scratch_shapes=[pltpu.VMEM((32, C), F32)],
        compiler_params=pltpu.CompilerParams(vmem_limit_bytes=16 * 2**20),
        name="pack",
    )(clip)
    k1, k2 = (kernel.reshape(3, 9, C, C) for kernel in (kernel_one, kernel_two))
    edge = lax.all_to_all(edge, "tm", 0, 0, tiled=True)
    v1, v2 = mixed_call(k1, k2)
    edge, mid, v1, v2 = lax.optimization_barrier((edge, mid, v1, v2))
    mid = lax.all_to_all(mid, "tm", 0, 0, tiled=True)
    me = lax.axis_index("rows")
    cross = lax.dynamic_slice_in_dim(edge, jnp.where(me == 7, 80, 0), 80, 1)
    cross = lax.ppermute(cross, "rows", [(7, 8), (8, 7)])
    above = lax.ppermute(edge[:, 80:], "rows", [(i, i + 1) for i in range(15) if i != 7])
    below = lax.ppermute(edge[:, :80], "rows", [(i + 1, i) for i in range(15) if i != 7])
    s = edges_call(above, edge, below, cross, gain_one, bias_one, gain_two, k1, v1)
    vectors = (gain_one, bias_one, gain_two, bias_two, down_bias)
    latent = block_call(edge, mid, vectors, down_kernel.reshape(3 * C, C), s, k1, v1, k2, v2)
    send = lax.all_to_all(latent, "tm", 0, 0, tiled=True)
    send = lax.all_to_all(send.reshape(16, 64, C), "rows", 0, 0, tiled=True)
    return send.reshape(1, 128, 8, C)


def solution(mesh):
    return jax.shard_map(
        body,
        mesh=mesh,
        in_specs=(P("tm", "rows", None, None), P(), P(), P(), P(), P(), P(), P(), P()),
        out_specs=P("tm", None, "rows", None),
        check_vma=False,
    )
```

```python
import jax
import jax.numpy as jnp
from jax import lax
from jax.experimental import pallas as pl
from jax.experimental.pallas import tpu as pltpu
from jax.sharding import PartitionSpec as P

EPS = 1e-06
C = 384
BF = jnp.bfloat16
F32 = jnp.float32


def activate(value, gain):
    square = jnp.mean(value * value, axis=-1, keepdims=True)
    scaled = value * lax.rsqrt(square + EPS) * gain
    half = 0.5 * scaled
    return half + half * jnp.tanh(half)


def earlier(value):
    rank = value.ndim
    index = lax.broadcasted_iota(jnp.int32, value.shape, rank - 2)
    return jnp.where(index == 0, 0.0, pltpu.roll(value, 1, rank - 2))


def transformed(even, odd):
    even_before, odd_before = earlier(even), earlier(odd)
    return even_before - even, odd_before + even, even - odd_before, odd_before - odd


GROUPS = (((0, 1), 0, 0), ((2, 3), 1, 0), ((4, 5), 1, 80), ((6, 7), 0, 80))


def pack_body(clip_ref, edge_ref, mid_ref, halo_ref):
    zero = jnp.zeros((2, C), F32)
    for d in range(8):
        for rows, which, base in GROUPS:
            out_ref = (edge_ref, mid_ref)[which]
            count = 2 * len(rows)
            for k in range(count):
                f, r = k // len(rows), rows[k % len(rows)]
                out_ref[d, base + 16 * k : base + 16 * k + 16] = clip_ref[f, r, 16 * d : 16 * d + 16]
                left, right = zero, zero
                if d > 0:
                    left = clip_ref[f, r, 16 * d - 16 : 16 * d].astype(F32)[14:16]
                if d < 7:
                    right = clip_ref[f, r, 16 * d + 16 : 16 * d + 32].astype(F32)[0:2]
                halo_ref[4 * k : 4 * k + 2] = left
                halo_ref[4 * k + 2 : 4 * k + 4] = right
            start = base + 16 * count
            out_ref[d, start : start + 4 * count] = halo_ref[0 : 4 * count].astype(BF)


VMEM_LIMIT = 60 * 2**20


def fetch(k_hbm, v_hbm, u_ref, sems, first):
    pairs = ((k_hbm.at[0], u_ref.at[0]), (v_hbm, u_ref.at[1:3]), (k_hbm.at[2], u_ref.at[3]))
    return [
        pltpu.make_async_copy(source, target, sems.at[first + n])
        for n, (source, target) in enumerate(pairs)
    ]


def reordered(source_of):
    place = lax.broadcasted_iota(jnp.int32, (256, 256), 0)
    source = lax.broadcasted_iota(jnp.int32, (256, 256), 1)
    return jnp.where(source_of(place) == source, 1.0, 0.0).astype(BF)


def unpack(x_ref, chunks):
    order = reordered(lambda k: (k // 128) * 128 + (k % 8) * 16 + (k % 128) // 8)
    for n in range(0, len(chunks), 2):
        rows = [chunk(source) for chunk in chunks[n : n + 2] for source in range(8)]
        moved = jnp.dot(order, jnp.concatenate(rows, axis=0), preferred_element_type=F32)
        x_ref[16 * n : 16 * n + 32] = moved.reshape(32, 8, C)


def chunks_of(ref, first, last):
    return [lambda source, at=at: ref[source, at : at + 16] for at in range(first, last, 16)]


def chosen(condition, ref, other_ref):
    return [
        lambda source, at=at: jnp.where(condition, ref[source, at : at + 16], other_ref[source, at : at + 16])
        for at in range(0, 80, 16)
    ]


def cells(x_ref, r, parity, halo):
    line = 2 * parity + r % 2
    main = x_ref[pl.ds(80 * (r // 2) + 16 * line, 16)]
    if not halo:
        return main
    at = 80 * (r // 2) + 64 + 4 * line
    return jnp.concatenate([x_ref[pl.ds(at, 2)], main, x_ref[pl.ds(at + 2, 2)]], axis=0)


def prepare_one(x_ref, d_ref, g1):
    def one(r, carry):
        halves = [
            activate(cells(x_ref, r, parity, True), g1).astype(BF).astype(F32)
            for parity in range(2)
        ]
        for q, d in enumerate(transformed(*halves)):
            d_ref[q, r] = jnp.concatenate([d[0:11], d[9:20]], axis=1).astype(BF)
        return carry

    lax.fori_loop(0, 8, one, 0)


def products(d_ref, u_ref, r, rows, width, arrivals=()):
    m = []
    count = rows * width * 16
    for q in range(4):
        for when, copy in arrivals:
            if when == q:
                copy.wait()

        def piece(i, first, span):
            return d_ref[q, pl.ds(r + i, rows), first : first + span].reshape(rows * span * 16, C)

        taps = [(i, j) for i in range(3) for j in range(3)]
        lhs = jnp.concatenate([piece(i, j, width) for i, j in taps], axis=1)
        main = jnp.dot(lhs, u_ref[q, :, :, :256].reshape(9 * C, 256), preferred_element_type=F32)
        lhs = jnp.concatenate([piece(i, 0, width + 1) for i in range(3)], axis=1)
        rhs = jnp.concatenate(
            [
                jnp.concatenate([u_ref[q, 3 * i + j, :, 256:] for j in range(2)], axis=1)
                for i in range(3)
            ],
            axis=0,
        )
        pair = jnp.dot(lhs, rhs, preferred_element_type=F32).reshape(rows, width + 1, 16, 256)
        lhs = jnp.concatenate([piece(i, 2, width) for i in range(3)], axis=1)
        rhs = jnp.concatenate([u_ref[q, 3 * i + 2, :, 256:] for i in range(3)], axis=0)
        last = jnp.dot(lhs, rhs, preferred_element_type=F32)
        rest = pair[:, :width, :, :128] + pair[:, 1:, :, 128:]
        m.append(jnp.concatenate([main, rest.reshape(count, 128) + last], axis=1))
    total, diff = m[1] + m[2], m[1] - m[2]
    return m[0] + total, diff - m[3]


def conv_one(d_ref, d_row, u_ref, b1, g2, s_ref, s_row, o, arrivals=()):
    col = lax.broadcasted_iota(jnp.int32, (2, 9, 8, 1), 1) + (lax.axis_index("tm") * 16 - 1)
    row = lax.broadcasted_iota(jnp.int32, (2, 9, 8, 1), 0) + (lax.axis_index("rows") * 8 - 1 + o)
    row_ok = (row >= 0) & (row < 128)
    for parity, h in enumerate(products(d_ref, u_ref, d_row, 2, 9, arrivals)):
        act = activate(h + b1, g2).reshape(2, 9, 2, 8, C)
        for half in range(2):
            column = col + 9 * half
            ok = row_ok & (column >= 0) & (column < 128)
            s_ref[parity, pl.ds(s_row, 2), 9 * half : 9 * half + 9] = jnp.where(ok, act[:, :, half], 0.0)


def edges_body(
    near_ref, edge_ref, far_ref, g1_ref, b1_ref, g2_ref, k1_hbm, v_hbm,
    s_ref, u1_ref, x_ref, d1_ref, sems,
):
    copies = fetch(k1_hbm, v_hbm.at[0:2], u1_ref, sems, 0)
    for copy in copies:
        copy.start()
    g1, b1, g2 = (ref[...].reshape(1, C) for ref in (g1_ref, b1_ref, g2_ref))
    even = lax.axis_index("rows") % 2 == 0
    unpack(
        x_ref,
        chosen(even, far_ref, near_ref) + chunks_of(edge_ref, 0, 160) + chosen(even, near_ref, far_ref),
    )
    prepare_one(x_ref, d1_ref, g1)
    arrivals = tuple(zip((0, 1, 3), copies))
    for block in range(2):
        conv_one(d1_ref, 4 * block, u1_ref, b1, g2, s_ref, 2 * block, 8 * block, arrivals)
        arrivals = ()


def block_body(
    edge_ref, mid_ref, g1_ref, b1_ref, g2_ref, b2_ref, db_ref,
    dk_hbm, s_hbm, k1_hbm, k2_hbm, v_hbm,
    out_ref, u1_ref, u2_ref, dk_ref, x_ref, d1_ref, d2_ref, s_ref, sems,
):
    copies_one = fetch(k1_hbm, v_hbm.at[0:2], u1_ref, sems, 0)
    copies_two = fetch(k2_hbm, v_hbm.at[2:4], u2_ref, sems, 3) + [
        pltpu.make_async_copy(dk_hbm, dk_ref, sems.at[6]),
        pltpu.make_async_copy(s_hbm.at[:, 0:2], s_ref.at[:, 0:2], sems.at[7]),
        pltpu.make_async_copy(s_hbm.at[:, 2:4], s_ref.at[:, 8:10], sems.at[8]),
    ]
    for copy in copies_one:
        copy.start()
    vectors = (g1_ref, b1_ref, g2_ref, b2_ref, db_ref)
    g1, b1, g2, b2, db = (ref[...].reshape(1, C) for ref in vectors)
    unpack(x_ref, chunks_of(edge_ref, 0, 80) + chunks_of(mid_ref, 0, 160) + chunks_of(edge_ref, 80, 160))
    order = reordered(lambda k: (k // 8 % 2) * 128 + (k % 8) * 16 + (k // 16 % 2) * 8 + k // 32)
    prepare_one(x_ref, d1_ref, g1)
    conv_one(d1_ref, 0, u1_ref, b1, g2, s_ref, 2, 2, tuple(zip((0, 1, 3), copies_one)))
    for copy in copies_two:
        copy.start()

    def step_one(block, carry):
        conv_one(d1_ref, 2 * block, u1_ref, b1, g2, s_ref, 2 * block + 2, 2 * block + 2)
        return carry

    lax.fori_loop(1, 3, step_one, 0)
    for copy in copies_two:
        copy.wait()

    def prepare_two(r, carry):
        for q, d in enumerate(transformed(s_ref[0, r], s_ref[1, r])):
            d2_ref[q, r] = jnp.concatenate([d[0:10], d[8:18]], axis=1).astype(BF)
        return carry

    lax.fori_loop(0, 10, prepare_two, 0)

    def step_two(block, carry):
        r = block * 2
        blocks = []
        for parity, h in enumerate(products(d2_ref, u2_ref, r, 2, 8)):
            part = jnp.stack([cells(x_ref, r + k, parity, False) for k in range(2)])
            part = jnp.concatenate([part[:, 0:8], part[:, 8:16]], axis=2).reshape(256, C)
            blocks.append((h + b2 + part).astype(BF).astype(F32))
        even, odd = blocks
        before = earlier(odd.reshape(32, 8, C)).reshape(256, C)
        lhs = jnp.concatenate([before.astype(BF), even.astype(BF), odd.astype(BF)], axis=1)
        latent = jnp.dot(lhs, dk_ref[...], preferred_element_type=F32) + db
        latent = jnp.dot(order, latent.astype(BF), preferred_element_type=F32).astype(BF)
        for j in range(8):
            for half in range(2):
                at = pl.multiple_of(64 * half + 8 * r, 16)
                out_ref[j, pl.ds(at, 16)] = latent[32 * j + 16 * half : 32 * j + 16 * half + 16]
        return carry

    lax.fori_loop(0, 4, step_two, 0)


def mixed_body(k1_ref, k2_ref, v_ref):
    for first, k_ref in ((0, k1_ref), (2, k2_ref)):
        for n in range(3):
            outer = 0.5 * (k_ref[0, n].astype(F32) + k_ref[2, n].astype(F32))
            middle = 0.5 * k_ref[1, n].astype(F32)
            v_ref[first, n] = (outer + middle).astype(BF)
            v_ref[first + 1, n] = (outer - middle).astype(BF)


def mixed_call(k1, k2):
    return pl.pallas_call(
        mixed_body,
        grid=(3,),
        out_shape=jax.ShapeDtypeStruct((4, 9, C, C), BF),
        in_specs=[pl.BlockSpec((3, 3, C, C), lambda n: (0, n, 0, 0))] * 2,
        out_specs=pl.BlockSpec((4, 3, C, C), lambda n: (0, n, 0, 0)),
        compiler_params=pltpu.CompilerParams(vmem_limit_bytes=VMEM_LIMIT),
        cost_estimate=pl.CostEstimate(flops=16000000, bytes_accessed=27000000, transcendentals=0),
        name="mixed",
    )(k1, k2)


VMEM = pl.BlockSpec(memory_space=pltpu.VMEM)
HBM = pl.BlockSpec(memory_space=pl.ANY)


def edges_call(near, edge, far, g1, b1, g2, k1, v):
    return pl.pallas_call(
        edges_body,
        out_shape=jax.ShapeDtypeStruct((2, 4, 18, 8, C), F32),
        in_specs=[VMEM] * 6 + [HBM] * 2,
        out_specs=VMEM,
        scratch_shapes=[
            pltpu.VMEM((4, 9, C, C), BF),
            pltpu.VMEM((320, 8, C), F32),
            pltpu.VMEM((4, 8, 11, 16, C), BF),
            pltpu.SemaphoreType.DMA((3,)),
        ],
        compiler_params=pltpu.CompilerParams(vmem_limit_bytes=54 * 2**20),
        cost_estimate=pl.CostEstimate(flops=10**10, bytes_accessed=15000000, transcendentals=0),
        name="edges",
    )(near, edge, far, g1, b1, g2, k1, v)


def block_call(edge, mid, vectors, dk, s, k1, k2, v):
    return pl.pallas_call(
        block_body,
        out_shape=jax.ShapeDtypeStruct((8, 128, C), BF),
        in_specs=[VMEM] * 7 + [HBM] * 5,
        out_specs=VMEM,
        scratch_shapes=[
            pltpu.VMEM((4, 9, C, C), BF),
            pltpu.VMEM((4, 9, C, C), BF),
            pltpu.VMEM((3 * C, C), BF),
            pltpu.VMEM((320, 8, C), F32),
            pltpu.VMEM((4, 8, 11, 16, C), BF),
            pltpu.VMEM((4, 10, 10, 16, C), BF),
            pltpu.VMEM((2, 10, 18, 8, C), F32),
            pltpu.SemaphoreType.DMA((9,)),
        ],
        compiler_params=pltpu.CompilerParams(vmem_limit_bytes=54 * 2**20),
        cost_estimate=pl.CostEstimate(flops=3 * 10**10, bytes_accessed=28000000, transcendentals=0),
        name="block",
    )(edge, mid, *vectors, dk, s, k1, k2, v)


def body(
    clip, gain_one, bias_one, kernel_one, gain_two, bias_two, kernel_two, down_kernel, down_bias
):
    edge, mid = pl.pallas_call(
        pack_body,
        out_shape=[jax.ShapeDtypeStruct((8, 160, C), BF)] * 2,
        in_specs=[VMEM],
        out_specs=[VMEM] * 2,
        scratch_shapes=[pltpu.VMEM((32, C), F32)],
        compiler_params=pltpu.CompilerParams(vmem_limit_bytes=16 * 2**20),
        name="pack",
    )(clip)
    k1, k2 = (kernel.reshape(3, 9, C, C) for kernel in (kernel_one, kernel_two))
    edge = lax.all_to_all(edge, "tm", 0, 0, tiled=True)
    v = mixed_call(k1, k2)
    edge, mid, v = lax.optimization_barrier((edge, mid, v))
    mid = lax.all_to_all(mid, "tm", 0, 0, tiled=True)
    odd = lax.axis_index("rows") % 2
    far = lax.dynamic_slice_in_dim(edge, 80 * odd, 80, 1)
    near = lax.dynamic_slice_in_dim(edge, 80 - 80 * odd, 80, 1)
    far_pairs = [(m, m + 1) for m in range(1, 15, 2)] + [(m + 1, m) for m in range(1, 15, 2)]
    near_pairs = [(m, m + 1) for m in range(0, 16, 2)] + [(m + 1, m) for m in range(0, 16, 2)]
    far = lax.ppermute(far, "rows", far_pairs)
    near = lax.ppermute(near, "rows", near_pairs)
    s = edges_call(near, edge, far, gain_one, bias_one, gain_two, k1, v)
    vectors = (gain_one, bias_one, gain_two, bias_two, down_bias)
    latent = block_call(edge, mid, vectors, down_kernel.reshape(3 * C, C), s, k1, k2, v)
    send = lax.all_to_all(latent, "tm", 0, 0, tiled=True)
    send = lax.all_to_all(send.reshape(16, 64, C), "rows", 0, 0, tiled=True)
    return send.reshape(1, 128, 8, C)


def solution(mesh):
    return jax.shard_map(
        body,
        mesh=mesh,
        in_specs=(P("tm", "rows", None, None), P(), P(), P(), P(), P(), P(), P(), P()),
        out_specs=P("tm", None, "rows", None),
        check_vma=False,
    )
```

```python
import jax
import jax.numpy as jnp
from jax import lax
from jax.experimental import pallas as pl
from jax.experimental.pallas import tpu as pltpu
from jax.sharding import PartitionSpec as P

EPS = 1e-06
C = 384
BF = jnp.bfloat16
F32 = jnp.float32


def activate(value, gain):
    square = jnp.mean(value * value, axis=-1, keepdims=True)
    scaled = value * lax.rsqrt(square + EPS) * gain
    half = 0.5 * scaled
    return half + half * jnp.tanh(half)


def earlier(value):
    rank = value.ndim
    index = lax.broadcasted_iota(jnp.int32, value.shape, rank - 2)
    return jnp.where(index == 0, 0.0, pltpu.roll(value, 1, rank - 2))


def transformed(even, odd):
    even_before, odd_before = earlier(even), earlier(odd)
    return even_before - even, odd_before + even, even - odd_before, odd_before - odd


GROUPS = (((0, 1), 0, 0), ((2, 3), 1, 0), ((4, 5), 1, 80), ((6, 7), 0, 80))


def pack_body(clip_ref, edge_ref, mid_ref, halo_ref):
    zero = jnp.zeros((2, C), F32)
    for d in range(8):
        for rows, which, base in GROUPS:
            out_ref = (edge_ref, mid_ref)[which]
            count = 2 * len(rows)
            for k in range(count):
                f, r = k // len(rows), rows[k % len(rows)]
                out_ref[d, base + 16 * k : base + 16 * k + 16] = clip_ref[f, r, 16 * d : 16 * d + 16]
                left, right = zero, zero
                if d > 0:
                    left = clip_ref[f, r, 16 * d - 16 : 16 * d].astype(F32)[14:16]
                if d < 7:
                    right = clip_ref[f, r, 16 * d + 16 : 16 * d + 32].astype(F32)[0:2]
                halo_ref[4 * k : 4 * k + 2] = left
                halo_ref[4 * k + 2 : 4 * k + 4] = right
            start = base + 16 * count
            out_ref[d, start : start + 4 * count] = halo_ref[0 : 4 * count].astype(BF)


VMEM_LIMIT = 60 * 2**20


def fetch(k_hbm, v_hbm, u_ref, sems, first):
    pairs = ((k_hbm.at[0], u_ref.at[0]), (v_hbm, u_ref.at[1:3]), (k_hbm.at[2], u_ref.at[3]))
    return [
        pltpu.make_async_copy(source, target, sems.at[first + n])
        for n, (source, target) in enumerate(pairs)
    ]


def reordered(source_of):
    place = lax.broadcasted_iota(jnp.int32, (256, 256), 0)
    source = lax.broadcasted_iota(jnp.int32, (256, 256), 1)
    return jnp.where(source_of(place) == source, 1.0, 0.0).astype(BF)


def unpack(x_ref, chunks):
    order = reordered(lambda k: (k // 128) * 128 + (k % 8) * 16 + (k % 128) // 8)
    for n in range(0, len(chunks), 2):
        rows = [chunk(source) for chunk in chunks[n : n + 2] for source in range(8)]
        moved = jnp.dot(order, jnp.concatenate(rows, axis=0), preferred_element_type=F32)
        x_ref[16 * n : 16 * n + 32] = moved.reshape(32, 8, C)


def chunks_of(ref, first, last):
    return [lambda source, at=at: ref[source, at : at + 16] for at in range(first, last, 16)]


def chosen(condition, ref, other_ref):
    return [
        lambda source, at=at: jnp.where(condition, ref[source, at : at + 16], other_ref[source, at : at + 16])
        for at in range(0, 80, 16)
    ]


def cells(x_ref, r, parity, halo):
    line = 2 * parity + r % 2
    main = x_ref[pl.ds(80 * (r // 2) + 16 * line, 16)]
    if not halo:
        return main
    at = 80 * (r // 2) + 64 + 4 * line
    return jnp.concatenate([x_ref[pl.ds(at, 2)], main, x_ref[pl.ds(at + 2, 2)]], axis=0)


def prepare_one(x_ref, d_ref, g1):
    def one(r, carry):
        halves = [
            activate(cells(x_ref, r, parity, True), g1).astype(BF).astype(F32)
            for parity in range(2)
        ]
        for q, d in enumerate(transformed(*halves)):
            d_ref[q, r] = jnp.concatenate([d[0:11], d[9:20]], axis=1).astype(BF)
        return carry

    lax.fori_loop(0, 8, one, 0)


def products(d_ref, u_ref, r, rows, width, arrivals=()):
    m = []
    count = rows * width * 16
    for q in range(4):
        for when, copy in arrivals:
            if when == q:
                copy.wait()

        def piece(i, first, span):
            return d_ref[q, pl.ds(r + i, rows), first : first + span].reshape(rows * span * 16, C)

        taps = [(i, j) for i in range(3) for j in range(3)]
        lhs = jnp.concatenate([piece(i, j, width) for i, j in taps], axis=1)
        main = jnp.dot(lhs, u_ref[q, :, :, :256].reshape(9 * C, 256), preferred_element_type=F32)
        lhs = jnp.concatenate([piece(i, 0, width + 1) for i in range(3)], axis=1)
        rhs = jnp.concatenate(
            [
                jnp.concatenate([u_ref[q, 3 * i + j, :, 256:] for j in range(2)], axis=1)
                for i in range(3)
            ],
            axis=0,
        )
        pair = jnp.dot(lhs, rhs, preferred_element_type=F32).reshape(rows, width + 1, 16, 256)
        lhs = jnp.concatenate([piece(i, 2, width) for i in range(3)], axis=1)
        rhs = jnp.concatenate([u_ref[q, 3 * i + 2, :, 256:] for i in range(3)], axis=0)
        last = jnp.dot(lhs, rhs, preferred_element_type=F32)
        rest = pair[:, :width, :, :128] + pair[:, 1:, :, 128:]
        m.append(jnp.concatenate([main, rest.reshape(count, 128) + last], axis=1))
    total, diff = m[1] + m[2], m[1] - m[2]
    return m[0] + total, diff - m[3]


def conv_one(d_ref, d_row, u_ref, b1, g2, s_ref, s_row, o, arrivals=()):
    col = lax.broadcasted_iota(jnp.int32, (2, 9, 8, 1), 1) + (lax.axis_index("tm") * 16 - 1)
    row = lax.broadcasted_iota(jnp.int32, (2, 9, 8, 1), 0) + (lax.axis_index("rows") * 8 - 1 + o)
    row_ok = (row >= 0) & (row < 128)
    for parity, h in enumerate(products(d_ref, u_ref, d_row, 2, 9, arrivals)):
        act = activate(h + b1, g2).reshape(2, 9, 2, 8, C)
        for half in range(2):
            column = col + 9 * half
            ok = row_ok & (column >= 0) & (column < 128)
            s_ref[parity, pl.ds(s_row, 2), 9 * half : 9 * half + 9] = jnp.where(ok, act[:, :, half], 0.0)


def edges_body(
    near_ref, edge_ref, far_ref, g1_ref, b1_ref, g2_ref, k1_hbm, v_hbm,
    s_ref, u1_ref, x_ref, d1_ref, sems,
):
    copies = fetch(k1_hbm, v_hbm.at[0:2], u1_ref, sems, 0)
    for copy in copies:
        copy.start()
    g1, b1, g2 = (ref[...].reshape(1, C) for ref in (g1_ref, b1_ref, g2_ref))
    even = lax.axis_index("rows") % 2 == 0
    unpack(
        x_ref,
        chosen(even, far_ref, near_ref) + chunks_of(edge_ref, 0, 160) + chosen(even, near_ref, far_ref),
    )
    prepare_one(x_ref, d1_ref, g1)
    arrivals = tuple(zip((0, 1, 3), copies))
    for block in range(2):
        conv_one(d1_ref, 4 * block, u1_ref, b1, g2, s_ref, 2 * block, 8 * block, arrivals)
        arrivals = ()


def block_body(
    edge_ref, mid_ref, g1_ref, b1_ref, g2_ref, b2_ref, db_ref,
    dk_hbm, s_hbm, k1_hbm, k2_hbm, v_hbm,
    out_ref, u1_ref, u2_ref, dk_ref, x_ref, d1_ref, d2_ref, s_ref, sems,
):
    copies_one = fetch(k1_hbm, v_hbm.at[0:2], u1_ref, sems, 0)
    copies_two = fetch(k2_hbm, v_hbm.at[2:4], u2_ref, sems, 3) + [
        pltpu.make_async_copy(dk_hbm, dk_ref, sems.at[6]),
        pltpu.make_async_copy(s_hbm.at[:, 0:2], s_ref.at[:, 0:2], sems.at[7]),
        pltpu.make_async_copy(s_hbm.at[:, 2:4], s_ref.at[:, 8:10], sems.at[8]),
    ]
    for copy in copies_one:
        copy.start()
    vectors = (g1_ref, b1_ref, g2_ref, b2_ref, db_ref)
    g1, b1, g2, b2, db = (ref[...].reshape(1, C) for ref in vectors)
    unpack(x_ref, chunks_of(edge_ref, 0, 80) + chunks_of(mid_ref, 0, 160) + chunks_of(edge_ref, 80, 160))
    order = reordered(lambda k: (k // 8 % 2) * 128 + (k % 8) * 16 + (k // 16 % 2) * 8 + k // 32)
    prepare_one(x_ref, d1_ref, g1)
    conv_one(d1_ref, 0, u1_ref, b1, g2, s_ref, 2, 2, tuple(zip((0, 1, 3), copies_one)))
    for copy in copies_two:
        copy.start()

    def step_one(block, carry):
        conv_one(d1_ref, 2 * block, u1_ref, b1, g2, s_ref, 2 * block + 2, 2 * block + 2)
        return carry

    lax.fori_loop(1, 3, step_one, 0)
    for copy in copies_two:
        copy.wait()

    def prepare_two(r, carry):
        for q, d in enumerate(transformed(s_ref[0, r], s_ref[1, r])):
            d2_ref[q, r] = jnp.concatenate([d[0:10], d[8:18]], axis=1).astype(BF)
        return carry

    lax.fori_loop(0, 10, prepare_two, 0)

    def step_two(block, carry):
        r = block * 2
        blocks = []
        for parity, h in enumerate(products(d2_ref, u2_ref, r, 2, 8)):
            part = jnp.stack([cells(x_ref, r + k, parity, False) for k in range(2)])
            part = jnp.concatenate([part[:, 0:8], part[:, 8:16]], axis=2).reshape(256, C)
            blocks.append((h + b2 + part).astype(BF).astype(F32))
        even, odd = blocks
        before = earlier(odd.reshape(32, 8, C)).reshape(256, C)
        lhs = jnp.concatenate([before.astype(BF), even.astype(BF), odd.astype(BF)], axis=1)
        latent = jnp.dot(lhs, dk_ref[...], preferred_element_type=F32) + db
        latent = jnp.dot(order, latent.astype(BF), preferred_element_type=F32).astype(BF)
        for j in range(8):
            for half in range(2):
                at = pl.multiple_of(64 * half + 8 * r, 16)
                out_ref[j, pl.ds(at, 16)] = latent[32 * j + 16 * half : 32 * j + 16 * half + 16]
        return carry

    lax.fori_loop(0, 4, step_two, 0)


def mixed_body(k1_ref, k2_ref, v_ref):
    for first, k_ref in ((0, k1_ref), (2, k2_ref)):
        for n in range(3):
            outer = 0.5 * (k_ref[0, n].astype(F32) + k_ref[2, n].astype(F32))
            middle = 0.5 * k_ref[1, n].astype(F32)
            v_ref[first, n] = (outer + middle).astype(BF)
            v_ref[first + 1, n] = (outer - middle).astype(BF)


def mixed_call(k1, k2):
    return pl.pallas_call(
        mixed_body,
        grid=(3,),
        out_shape=jax.ShapeDtypeStruct((4, 9, C, C), BF),
        in_specs=[pl.BlockSpec((3, 3, C, C), lambda n: (0, n, 0, 0))] * 2,
        out_specs=pl.BlockSpec((4, 3, C, C), lambda n: (0, n, 0, 0)),
        compiler_params=pltpu.CompilerParams(vmem_limit_bytes=VMEM_LIMIT),
        cost_estimate=pl.CostEstimate(flops=16000000, bytes_accessed=27000000, transcendentals=0),
        name="mixed",
    )(k1, k2)


VMEM = pl.BlockSpec(memory_space=pltpu.VMEM)
HBM = pl.BlockSpec(memory_space=pl.ANY)


def edges_call(near, edge, far, g1, b1, g2, k1, v):
    return pl.pallas_call(
        edges_body,
        out_shape=jax.ShapeDtypeStruct((2, 4, 18, 8, C), F32),
        in_specs=[VMEM] * 6 + [HBM] * 2,
        out_specs=VMEM,
        scratch_shapes=[
            pltpu.VMEM((4, 9, C, C), BF),
            pltpu.VMEM((320, 8, C), F32),
            pltpu.VMEM((4, 8, 11, 16, C), BF),
            pltpu.SemaphoreType.DMA((3,)),
        ],
        compiler_params=pltpu.CompilerParams(vmem_limit_bytes=50 * 2**20),
        cost_estimate=pl.CostEstimate(flops=10**10, bytes_accessed=15000000, transcendentals=0),
        name="edges",
    )(near, edge, far, g1, b1, g2, k1, v)


def block_call(edge, mid, vectors, dk, s, k1, k2, v):
    return pl.pallas_call(
        block_body,
        out_shape=jax.ShapeDtypeStruct((8, 128, C), BF),
        in_specs=[VMEM] * 7 + [HBM] * 5,
        out_specs=VMEM,
        scratch_shapes=[
            pltpu.VMEM((4, 9, C, C), BF),
            pltpu.VMEM((4, 9, C, C), BF),
            pltpu.VMEM((3 * C, C), BF),
            pltpu.VMEM((320, 8, C), F32),
            pltpu.VMEM((4, 8, 11, 16, C), BF),
            pltpu.VMEM((4, 10, 10, 16, C), BF),
            pltpu.VMEM((2, 10, 18, 8, C), F32),
            pltpu.SemaphoreType.DMA((9,)),
        ],
        compiler_params=pltpu.CompilerParams(vmem_limit_bytes=50 * 2**20),
        cost_estimate=pl.CostEstimate(flops=3 * 10**10, bytes_accessed=28000000, transcendentals=0),
        name="block",
    )(edge, mid, *vectors, dk, s, k1, k2, v)


def body(
    clip, gain_one, bias_one, kernel_one, gain_two, bias_two, kernel_two, down_kernel, down_bias
):
    edge, mid = pl.pallas_call(
        pack_body,
        out_shape=[jax.ShapeDtypeStruct((8, 160, C), BF)] * 2,
        in_specs=[VMEM],
        out_specs=[VMEM] * 2,
        scratch_shapes=[pltpu.VMEM((32, C), F32)],
        compiler_params=pltpu.CompilerParams(vmem_limit_bytes=16 * 2**20),
        name="pack",
    )(clip)
    k1, k2 = (kernel.reshape(3, 9, C, C) for kernel in (kernel_one, kernel_two))
    edge = lax.all_to_all(edge, "tm", 0, 0, tiled=True)
    v = mixed_call(k1, k2)
    edge, mid, v = lax.optimization_barrier((edge, mid, v))
    mid = lax.all_to_all(mid, "tm", 0, 0, tiled=True)
    odd = lax.axis_index("rows") % 2
    far = lax.dynamic_slice_in_dim(edge, 80 * odd, 80, 1)
    near = lax.dynamic_slice_in_dim(edge, 80 - 80 * odd, 80, 1)
    far_pairs = [(m, m + 1) for m in range(1, 15, 2)] + [(m + 1, m) for m in range(1, 15, 2)]
    near_pairs = [(m, m + 1) for m in range(0, 16, 2)] + [(m + 1, m) for m in range(0, 16, 2)]
    far = lax.ppermute(far, "rows", far_pairs)
    near = lax.ppermute(near, "rows", near_pairs)
    s = edges_call(near, edge, far, gain_one, bias_one, gain_two, k1, v)
    vectors = (gain_one, bias_one, gain_two, bias_two, down_bias)
    latent = block_call(edge, mid, vectors, down_kernel.reshape(3 * C, C), s, k1, k2, v)
    send = lax.all_to_all(latent, "tm", 0, 0, tiled=True)
    send = lax.all_to_all(send.reshape(16, 64, C), "rows", 0, 0, tiled=True)
    return send.reshape(1, 128, 8, C)


def solution(mesh):
    return jax.shard_map(
        body,
        mesh=mesh,
        in_specs=(P("tm", "rows", None, None), P(), P(), P(), P(), P(), P(), P(), P()),
        out_specs=P("tm", None, "rows", None),
        check_vma=False,
    )
```
